32 devices in a mesh: rep: 2 (over y), dom: 4 (over z), slab: 2 (over x), half: 2 (over core).
Axes of the slice: x: 2, y: 2, z: 4, core: 2. Of those that a mesh axis runs over, the one named last changes fastest.
Arguments:
- leaf_multipoles: bfloat16 [81, 8192], P(None, ('rep', 'dom', 'slab', 'half')), parts along dimension 1, may hold values from -6 to 6
- translate: bfloat16 [316, 81, 81], replicated, may hold values from -0.0390625 to 0.0390625
- shift_up: bfloat16 [8, 81, 81], replicated, may hold values from -0.25 to 0.25
- shift_down: bfloat16 [8, 81, 81], replicated, may hold values from -0.625 to 0.625
- export_rows: int32 [32, 16, 32], P(('rep', 'dom', 'slab', 'half')), parts along dimension 0, may hold values from 0 to 255
- leaf_lists: int32 [316, 8192], P(None, ('rep', 'dom', 'slab', 'half')), parts along dimension 1, may hold values from 0 to 768, as said below
- coarse_lists: int32 [316, 1024], P(None, ('rep', 'dom', 'slab', 'half')), parts along dimension 1, may hold values from 0 to 512, as said below
- positions: float32 [3, 131072], P(None, ('rep', 'dom', 'slab', 'half')), parts along dimension 1, may hold values from 0 to 1
- charges: float32 [131072], P(('rep', 'dom', 'slab', 'half')), parts along dimension 0, may hold values from -0.3 to 0.3
- counts: int32 [8192], P(('rep', 'dom', 'slab', 'half')), parts along dimension 0, may hold values from 1 to 16
- near_lists: int32 [27, 8192], P(None, ('rep', 'dom', 'slab', 'half')), parts along dimension 1, may hold values from 0 to 288, as said below
Outputs:
- local_field: float32 [81, 8192], P(None, ('rep', 'dom', 'slab', 'half')), parts along dimension 1
- near_potential: float32 [131072], P(('rep', 'dom', 'slab', 'half')), parts along dimension 0
The draws below stay inside these ranges and needn't reach their ends.
There are 2 independent parts, one for each index of `rep`. The reference program is written for one: setup_inputs(seed, part) draws one part's arguments, and reference() takes and returns one part's arrays. A program takes and returns all parts, laid end to end along the dimension named above; an argument that names none is the same for every part. Nothing has to cross between parts.
Inputs may be any that keep to these rules, and one draw needn't show every extreme that they name: `leaf_lists`: each device's entries are relative to that device; an imported entry of device r names a peer p with (p - r) mod 16 in 1 to 8 or in 8 to 15; 768 means no source. `coarse_lists`: 512 means no source. `near_lists`: each entry lies within 16 boxes of its target's local index shifted by 16, or is 288 for no tile.
All inputs are finite; a program needn't handle non-finite values.
Results may differ from the reference program's by a relative error of at most 0.0019.
Values may be sent and summed in bfloat16 or wider, within the bound.
A program may use at most 128 MiB of HBM per device.

```python
import jax
import jax.numpy as jnp
from jax import lax

NCOEF = 81
NOFF = 316
NNEAR = 27
HALO = 16
BOX_DEV = 256
SLOTS = 16
CAP = 32
PEERS = 16
NBR = 8
BOXES = 4096
CBOXES = 512


def draw_leaf_lists(key, part):
    key = jax.random.fold_in(key, 11)
    first, second, third, fourth, fifth = jax.random.split(key, 5)
    shape = (NOFF, BOXES)
    pick = jax.random.randint(first, shape, 0, 10)
    local = jax.random.randint(second, shape, 0, BOX_DEV)
    owner = jnp.arange(BOXES, dtype=jnp.int32) // BOX_DEV
    reach = jax.random.randint(third, shape, 1, NBR + 1)
    side = 2 * jax.random.randint(fourth, shape, 0, 2) - 1
    peer = (owner[None, :] + side * reach) % PEERS
    slot = jax.random.randint(fifth, shape, 0, CAP)
    imported = BOX_DEV + peer * CAP + slot
    result = jnp.where(pick < 2, BOX_DEV + PEERS * CAP, jnp.where(pick < 4, local, imported))
    far_peer = (owner + PEERS // 2) % PEERS
    far_entry = BOX_DEV + far_peer * CAP + owner % CAP
    first_box = jnp.arange(BOXES, dtype=jnp.int32) % BOX_DEV == 0
    result = result.at[2].set(jnp.where(first_box, far_entry, result[2]))
    result = result.at[0, 0].set(BOX_DEV + PEERS * CAP).at[1, 0].set(0)
    return result.astype(jnp.int32)


def draw_coarse_lists(key, part):
    key = jax.random.fold_in(key, 23)
    first, second = jax.random.split(key, 2)
    shape = (NOFF, CBOXES)
    pick = jax.random.randint(first, shape, 0, 10)
    source = jax.random.randint(second, shape, 0, CBOXES)
    result = jnp.where(pick < 4, CBOXES, source)
    result = result.at[0, 0].set(CBOXES).at[1, 0].set(0)
    return result.astype(jnp.int32)


def draw_counts(key, part):
    key = jax.random.fold_in(key, 37)
    first, second = jax.random.split(key, 2)
    density = jax.random.randint(first, (PEERS, 1), 1, 5)
    base = jax.random.randint(second, (PEERS, BOX_DEV), 1, SLOTS // 4 + 1)
    result = jnp.minimum(base * density, SLOTS).reshape(BOXES)
    result = result.at[0].set(SLOTS)
    return result.astype(jnp.int32)


def draw_near_lists(key, part):
    key = jax.random.fold_in(key, 41)
    first, second = jax.random.split(key, 2)
    shape = (NNEAR, BOXES)
    local_index = jnp.arange(BOXES, dtype=jnp.int32) % BOX_DEV
    offset = jax.random.randint(first, shape, -HALO, HALO + 1)
    pick = jax.random.randint(second, shape, 0, 5)
    result = jnp.where(pick == 0, BOX_DEV + 2 * HALO, local_index[None, :] + HALO + offset)
    result = result.at[0, 0].set(BOX_DEV + 2 * HALO).at[1, 0].set(0)
    result = result.at[2, BOX_DEV - 1].set(BOX_DEV + 2 * HALO - 1)
    return result.astype(jnp.int32)


def set_ends(drawn, own_key, least, largest):
    shape = drawn.shape
    spot = [jax.random.randint(jax.random.fold_in(own_key, axis), (), 0, shape[axis]) for axis in range(len(shape))]
    drawn = drawn.at[tuple(spot)].set(least)
    longest = shape.index(max(shape))
    spot[longest] = (spot[longest] + 1) % shape[longest]
    return drawn.at[tuple(spot)].set(largest)


def block_scale(key, dims, pieces, least, high):
    def one(position, shards_of):
        heights = jax.random.uniform(jax.random.fold_in(jax.random.fold_in(key, 6), position), (shards_of,), jnp.float32, least / len(pieces), high / len(pieces))
        return jnp.repeat(jnp.exp(heights), dims[position] // shards_of).reshape((-1,) + (1,) * (len(dims) - position - 1))

    gain = one(*pieces[0])
    for cut in pieces[1:]:
        gain = gain * one(*cut)
    return gain


def noise(own_key, shape, scale, most, shards=(), kind=jnp.bfloat16):
    values = scale * jax.random.normal(own_key, shape, jnp.float32)
    if shards:
        values = values * block_scale(own_key, shape, shards, -0.22, 0.18)
    return jnp.clip(values, -most, most).astype(kind)


def setup_inputs(seed: int = 0, part: int = 0) -> dict:
    arg_keys = jax.random.split(jax.random.key(seed), 12)
    part_keys = jax.random.split(jax.random.fold_in(arg_keys[11], part), 12)
    return {
        "leaf_multipoles": noise(part_keys[0], (NCOEF, BOXES), 1.0, 6.0, ((1, 16),)),
        "translate": noise(arg_keys[1], (NOFF, NCOEF, NCOEF), (NCOEF * NOFF) ** -0.5, 0.0390625),
        "shift_up": noise(arg_keys[2], (8, NCOEF, NCOEF), (8 * NCOEF) ** -0.5, 0.25),
        "shift_down": noise(arg_keys[3], (8, NCOEF, NCOEF), NCOEF ** -0.5, 0.625),
        "export_rows": set_ends(jax.random.randint(part_keys[4], (PEERS, PEERS, CAP), 0, BOX_DEV), jax.random.fold_in(part_keys[4], 1), 0, BOX_DEV - 1).astype(jnp.int32),
        "leaf_lists": draw_leaf_lists(jax.random.fold_in(jax.random.fold_in(arg_keys[11], part), 71), part),
        "coarse_lists": draw_coarse_lists(jax.random.fold_in(jax.random.fold_in(arg_keys[11], part), 71), part),
        "positions": jnp.clip(1.0 * jax.random.uniform(part_keys[7], (3, BOXES * SLOTS), jnp.float32) ** block_scale(part_keys[7], (3, BOXES * SLOTS), ((1, 16),), -0.2, 0.2), 0.0, 1.0),
        "charges": noise(part_keys[8], (BOXES * SLOTS,), 0.05, 0.3, ((0, 16),), jnp.float32),
        "counts": draw_counts(jax.random.fold_in(jax.random.fold_in(arg_keys[11], part), 71), part),
        "near_lists": draw_near_lists(jax.random.fold_in(jax.random.fold_in(arg_keys[11], part), 71), part),
    }


softening = 0.01
best = lax.Precision.HIGHEST

def near_sum(extended, targets, rows):

    def step(total, index):
        source = extended[:, index, :]
        dist = jnp.zeros(total.shape + (source.shape[2],), jnp.float32)
        for axis_id in range(3):
            diff = targets[axis_id][:, :, None] - source[axis_id][:, None, :]
            dist = dist + diff * diff
        return (total + lax.optimization_barrier(jnp.sum(source[3][:, None, :] * lax.rsqrt(dist + softening), axis=2)), None)
    start = jnp.zeros(targets.shape[1:], jnp.float32)
    return lax.scan(step, start, rows)[0]

def reference(leaf_multipoles, translate, shift_up, shift_down, export_rows, leaf_lists, coarse_lists, positions, charges, counts, near_lists):
    wide = translate.astype(jnp.float32)
    mult_ext = jnp.concatenate([leaf_multipoles.astype(jnp.float32), jnp.zeros((NCOEF, 1), jnp.float32)], 1)

    def leaf_block(owner):
        lists = lax.dynamic_slice_in_dim(leaf_lists, owner * BOX_DEV, BOX_DEV, 1)
        imported = jnp.clip(lists - BOX_DEV, 0, PEERS * CAP - 1)
        peer = imported // CAP
        slot = imported % CAP
        remote = peer * BOX_DEV + export_rows[peer, owner, slot]
        target = jnp.where(lists < BOX_DEV, owner * BOX_DEV + lists, jnp.where(lists < BOX_DEV + PEERS * CAP, remote, BOXES))
        columns = mult_ext[:, target]
        return jnp.einsum('okc,cob->kb', wide, columns, precision=best)
    leaf_far = lax.map(leaf_block, jnp.arange(PEERS, dtype=jnp.int32))
    leaf_far = jnp.transpose(leaf_far, (1, 0, 2)).reshape(NCOEF, BOXES)
    children = leaf_multipoles.astype(jnp.float32).reshape(NCOEF, CBOXES, 8)
    parents = jnp.einsum('ckm,mpc->kp', shift_up.astype(jnp.float32), children, precision=best)
    parent_ext = jnp.concatenate([parents, jnp.zeros((NCOEF, 1), jnp.float32)], 1)
    coarse_dev = BOX_DEV // 8

    def coarse_block(owner):
        lists = lax.dynamic_slice_in_dim(coarse_lists, owner * coarse_dev, coarse_dev, 1)
        return jnp.einsum('okc,cob->kb', wide, parent_ext[:, lists], precision=best)
    coarse_local = lax.map(coarse_block, jnp.arange(PEERS, dtype=jnp.int32))
    coarse_local = jnp.transpose(coarse_local, (1, 0, 2)).reshape(NCOEF, CBOXES)
    coarse_round = coarse_local.astype(jnp.bfloat16).astype(jnp.float32)
    down = jnp.einsum('ckm,mp->kpc', shift_down.astype(jnp.float32), coarse_round, precision=best).reshape(NCOEF, BOXES)
    local_field = leaf_far + down
    valid = (jnp.arange(SLOTS, dtype=jnp.int32)[None, :] < counts[:, None]).astype(jnp.float32)
    q_eff = charges.reshape(BOXES, SLOTS) * valid
    packed = jnp.concatenate([positions, q_eff.reshape(1, BOXES * SLOTS)], 0)
    padded = jnp.pad(packed, ((0, 0), (HALO * SLOTS, HALO * SLOTS)))

    def near_block(owner):
        window = lax.dynamic_slice_in_dim(padded, owner * BOX_DEV * SLOTS, (BOX_DEV + 2 * HALO) * SLOTS, 1)
        extended = jnp.concatenate([window.reshape(4, BOX_DEV + 2 * HALO, SLOTS), jnp.zeros((4, 1, SLOTS), jnp.float32)], 1)
        targets = lax.dynamic_slice_in_dim(packed, owner * BOX_DEV * SLOTS, BOX_DEV * SLOTS, 1).reshape(4, BOX_DEV, SLOTS)
        rows = lax.dynamic_slice_in_dim(near_lists, owner * BOX_DEV, BOX_DEV, 1)
        mine = lax.dynamic_slice_in_dim(valid, owner * BOX_DEV, BOX_DEV, 0)
        return near_sum(extended, targets, rows) * mine
    near_potential = lax.map(near_block, jnp.arange(PEERS, dtype=jnp.int32)).reshape(BOXES * SLOTS)
    return (local_field, near_potential)
```

```python
import functools

import jax
import jax.numpy as jnp
from jax import lax
from jax.experimental import pallas as pl
from jax.experimental.pallas import tpu as pltpu
from jax.sharding import PartitionSpec as P

HALO = 16
CAP = 32
LANES = 128
WIDE = 256
ROWS = 88
STEP = 8

softening = 0.01
DEVICES = ("dom", "slab", "half")
f32 = jnp.float32
bf16 = jnp.bfloat16


def one_hot(row, width):
    picks = lax.broadcasted_iota(jnp.int32, (width, row.shape[1]), 0) == row
    return jnp.where(picks, 1.0, 0.0).astype(bf16)


def pick_block(stacked, block, first, stride, count):
    value = jnp.zeros((ROWS, stacked.shape[1]), f32)
    for j in range(count):
        start = first + j * stride
        value = jnp.where(block == j, stacked[start : start + ROWS], value)
    return value


def far_kernel(
    leaf_ref, arrived_ref, translate_ref, down_ref, lists_ref, clists_ref, out_ref,
    source_ref, parent_ref, matrix_ref, column_ref, acc_ref,
):
    coeffs, boxes = leaf_ref.shape
    offsets = translate_ref.shape[0]
    peers = arrived_ref.shape[0]
    together = WIDE // CAP
    groups = peers // together
    matrix_ref[...] = jnp.zeros_like(matrix_ref)
    acc_ref[...] = jnp.zeros_like(acc_ref)

    def turned(j, kind):
        part = arrived_ref[j * together : (j + 1) * together, kind * CAP : (kind + 1) * CAP, :]
        return jnp.transpose(part.reshape(WIDE, LANES).astype(f32))[:ROWS]

    own = jnp.concatenate([leaf_ref[...].astype(f32), jnp.zeros((ROWS - coeffs, boxes), f32)], 0)
    source_ref[...] = jnp.concatenate([own] + [turned(j, 0) for j in range(groups)], 0).astype(bf16)
    parent_ref[...] = jnp.concatenate(
        [turned(j, kind) for j in range(groups) for kind in (1, 2)], 0
    ).astype(bf16)
    lane_group = lax.broadcasted_iota(jnp.int32, (1, WIDE), 1) // (WIDE // STEP)
    fill = jnp.zeros((LANES - ROWS, WIDE), f32)

    def step(s, carry):
        row = clists_ref[s]
        rows = lists_ref[pl.ds(pl.multiple_of(s * STEP, STEP), STEP), :]
        found = jnp.dot(parent_ref[...], one_hot(row % WIDE, WIDE), preferred_element_type=f32)
        high = pick_block(found, row // WIDE, 0, 2 * ROWS, groups)
        low = pick_block(found, row // WIDE, ROWS, 2 * ROWS, groups)
        low = jnp.concatenate([low[:, LANES:], low[:, :LANES]], 1)
        for i in range(STEP):
            offset = s * STEP + i
            row = rows[i : i + 1]
            found = jnp.dot(source_ref[...], one_hot(row % WIDE, WIDE), preferred_element_type=f32)
            column = pick_block(found, row // WIDE, 0, ROWS, groups + 1)
            column_ref[LANES * i : LANES * (i + 1), :WIDE] = jnp.concatenate([column, fill], 0).astype(bf16)
            column = jnp.where(
                lane_group == i, high, jnp.where(lane_group == (i + STEP // 2) % STEP, low, 0.0)
            )
            column_ref[LANES * i : LANES * (i + 1), WIDE:] = jnp.concatenate([column, fill], 0).astype(bf16)
            matrix_ref[:coeffs, LANES * i : LANES * i + coeffs] = translate_ref[
                jnp.minimum(offset, offsets - 1)
            ]
        acc_ref[...] += jnp.dot(matrix_ref[...], column_ref[...], preferred_element_type=f32)
        return carry

    lax.fori_loop(0, clists_ref.shape[0], step, 0)
    coarse = acc_ref[:, WIDE : WIDE + LANES] + acc_ref[:, WIDE + LANES :]
    coarse = coarse + pltpu.roll(coarse, LANES // 2, 1)
    coarse = coarse + pltpu.roll(coarse, LANES // 4, 1)
    coarse_round = coarse.astype(bf16)
    box = lax.broadcasted_iota(jnp.int32, (LANES, boxes), 1)
    parent = lax.broadcasted_iota(jnp.int32, (LANES, boxes), 0)
    spread = jnp.dot(
        coarse_round, jnp.where(box // 8 == parent, 1.0, 0.0).astype(bf16), preferred_element_type=f32
    )[:coeffs]
    octant = lax.broadcasted_iota(jnp.int32, (1, boxes), 1) % 8
    total = acc_ref[:coeffs, :WIDE]
    for c in range(8):
        total = total + jnp.dot(
            down_ref[c], jnp.where(octant == c, spread, 0.0).astype(bf16), preferred_element_type=f32
        )
    out_ref[...] = total


def far_sum(leaf_multipoles, arrived, translate, shift_down, leaf_lists, coarse_lists):
    coeffs, boxes = leaf_multipoles.shape
    offsets, coarse = coarse_lists.shape
    assert boxes == WIDE and coarse * STEP == WIDE
    peers = arrived.shape[0]
    groups = peers * CAP // WIDE
    steps = -(-offsets // STEP)
    extra = ((0, steps * STEP - offsets), (0, 0))
    lists = jnp.pad(leaf_lists, extra, constant_values=boxes + peers * CAP)
    clists = jnp.pad(coarse_lists, extra, constant_values=peers * coarse).reshape(steps, 1, WIDE)
    return pl.pallas_call(
        far_kernel,
        out_shape=jax.ShapeDtypeStruct((coeffs, boxes), f32),
        in_specs=[pl.BlockSpec(memory_space=pltpu.VMEM)] * 6,
        out_specs=pl.BlockSpec(memory_space=pltpu.VMEM),
        scratch_shapes=[
            pltpu.VMEM(((groups + 1) * ROWS, WIDE), bf16),
            pltpu.VMEM((groups * 2 * ROWS, WIDE), bf16),
            pltpu.VMEM((ROWS, STEP * LANES), bf16),
            pltpu.VMEM((STEP * LANES, 2 * WIDE), bf16),
            pltpu.VMEM((ROWS, 2 * WIDE), f32),
        ],
        compiler_params=pltpu.CompilerParams(vmem_limit_bytes=40 * 2**20),
        name="far",
    )(leaf_multipoles, arrived, translate, shift_down, lists, clists)


def near_kernel(atoms_ref, edges_ref, lists_ref, counts_ref, out_ref):
    slots, boxes = out_ref.shape
    tiles = boxes // LANES

    def tile_sum(t):
        lanes = slice(t * LANES, (t + 1) * LANES)
        target = [atoms_ref[k * slots : (k + 1) * slots, lanes] for k in range(3)]

        def step(n, total):
            entry = lists_ref[n, :, lanes]
            local = entry - HALO
            inside = jnp.broadcast_to(local // LANES == t, (8, LANES)) & jnp.broadcast_to(local >= 0, (8, LANES))
            first = jnp.broadcast_to(local & (LANES - 1), (8, LANES))
            second = jnp.broadcast_to(local & (2 * HALO - 1), (8, LANES))
            source = []
            for r in range(4 * slots // 8):
                rows = slice(8 * r, 8 * (r + 1))
                one = jnp.take_along_axis(atoms_ref[rows, lanes], first, axis=1)
                two = jnp.take_along_axis(edges_ref[rows, lanes], second, axis=1)
                source.append(jnp.where(inside, one, two))
            source = jnp.concatenate(source, 0)
            present = entry < boxes + 2 * HALO
            charge = jnp.where(present, source[3 * slots :], 0.0)
            for b in range(slots):
                square = jnp.full((slots, LANES), softening, f32)
                for k in range(3):
                    diff = target[k] - source[k * slots + b : k * slots + b + 1]
                    square = square + diff * diff
                total = total + charge[b : b + 1] * lax.rsqrt(square)
            return total

        return lax.fori_loop(0, lists_ref.shape[0], step, jnp.zeros((slots, LANES), f32))

    slot = lax.broadcasted_iota(jnp.int32, (slots, LANES), 0)
    for t in range(tiles):
        lanes = slice(t * LANES, (t + 1) * LANES)
        out_ref[:, lanes] = jnp.where(slot < counts_ref[:, lanes], tile_sum(t), 0.0)


def near_part(positions, charges, counts, near_lists):
    boxes = counts.shape[0]
    slots = charges.shape[0] // boxes
    valid = jnp.arange(slots, dtype=jnp.int32)[:, None] < counts[None, :]
    charge = jnp.where(valid, charges.reshape(boxes, slots).T, 0.0)
    place = positions.reshape(3, boxes, slots).transpose(0, 2, 1).reshape(3 * slots, boxes)
    atoms = jnp.concatenate([place, charge], 0)
    count = lax.axis_size(DEVICES)
    forward = [(i, i + 1) for i in range(count - 1)]
    backward = [(target, source) for source, target in forward]
    below = lax.ppermute(atoms[:, boxes - HALO :], DEVICES, forward)
    above = lax.ppermute(atoms[:, :HALO], DEVICES, backward)
    fill = jnp.zeros((4 * slots, LANES - 2 * HALO), f32)
    edges = []
    for t in range(boxes // LANES):
        low, high = t * LANES, (t + 1) * LANES
        edges += [
            atoms[:, high : high + HALO] if high < boxes else above,
            atoms[:, low - HALO : low] if t else below,
            fill,
        ]
    potential = pl.pallas_call(
        near_kernel,
        out_shape=jax.ShapeDtypeStruct((slots, boxes), f32),
        in_specs=[pl.BlockSpec(memory_space=pltpu.VMEM)] * 4,
        out_specs=pl.BlockSpec(memory_space=pltpu.VMEM),
        name="near",
        cost_estimate=pl.CostEstimate(flops=40_000_000, bytes_accessed=2**18, transcendentals=0),
    )(atoms, jnp.concatenate(edges, 1), near_lists[:, None, :], counts[None, :])
    return potential.T.reshape(boxes * slots)


def far_part(leaf_multipoles, translate, shift_up, shift_down, export_rows, leaf_lists, coarse_lists):
    coeffs, boxes = leaf_multipoles.shape
    peers = export_rows.shape[1]
    exported = leaf_multipoles[:, export_rows[0].reshape(-1)].T.reshape(peers, CAP, coeffs)
    children = leaf_multipoles.reshape(coeffs, boxes // 8, 8)
    parents = jnp.einsum("ckm,mpc->pk", shift_up, children, preferred_element_type=f32)
    high = lax.reduce_precision(parents, 8, 7)
    both = jnp.concatenate([high, parents - high], 0).astype(bf16)
    outgoing = jnp.concatenate(
        [exported, jnp.broadcast_to(both[None], (peers,) + both.shape)], 1
    )
    outgoing = jnp.pad(outgoing, ((0, 0), (0, 0), (0, LANES - coeffs)))
    arrived = lax.all_to_all(outgoing, DEVICES, split_axis=0, concat_axis=0, tiled=True)
    return far_sum(leaf_multipoles, arrived, translate, shift_down, leaf_lists, coarse_lists)


def body(
    leaf_multipoles, translate, shift_up, shift_down, export_rows, leaf_lists, coarse_lists,
    positions, charges, counts, near_lists,
):
    local_field = far_part(
        leaf_multipoles, translate, shift_up, shift_down, export_rows, leaf_lists, coarse_lists
    )
    near_potential = near_part(positions, charges, counts, near_lists)
    return (local_field, near_potential)


def solution(mesh):
    every = ("rep",) + DEVICES
    in_specs = (
        P(None, every), P(), P(), P(), P(every, None, None), P(None, every), P(None, every),
        P(None, every), P(every), P(every), P(None, every),
    )
    out_specs = (P(None, every), P(every))
    return jax.shard_map(body, mesh=mesh, in_specs=in_specs, out_specs=out_specs, check_vma=False)
```

```python
import functools

import jax
import jax.numpy as jnp
from jax import lax
from jax.experimental import pallas as pl
from jax.experimental.pallas import tpu as pltpu
from jax.sharding import PartitionSpec as P

HALO = 16
CAP = 32
LANES = 128
WIDE = 256
ROWS = 88
STEP = 8

softening = 0.01
DEVICES = ("dom", "slab", "half")
f32 = jnp.float32
bf16 = jnp.bfloat16


def one_hot(row, width):
    numbers = lax.broadcasted_iota(jnp.int32, (width, row.shape[1]), 0).astype(f32).astype(bf16)
    picks = numbers == row.astype(f32).astype(bf16)
    return jnp.where(picks, jnp.ones((), bf16), jnp.zeros((), bf16))


def pick_block(stacked, block, first, stride, count):
    value = jnp.zeros((ROWS, stacked.shape[1]), f32)
    for j in range(count):
        start = first + j * stride
        value = jnp.where(block == j, stacked[start : start + ROWS], value)
    return value


def far_kernel(
    leaf_ref, arrived_ref, translate_ref, down_ref, lists_ref, clists_ref, out_ref,
    source_ref, parent_ref, matrix_ref, column_ref, acc_ref,
):
    coeffs, boxes = leaf_ref.shape
    offsets = translate_ref.shape[2]
    peers = arrived_ref.shape[0]
    together = WIDE // CAP
    groups = peers // together

    def turn(k, carry):
        rows = jnp.concatenate(
            [translate_ref[k].astype(f32), jnp.zeros((LANES - coeffs, offsets), f32)], 0
        )
        matrix_ref[pl.ds(k, offsets, stride=ROWS), :] = jnp.transpose(rows)
        return carry

    lax.fori_loop(0, coeffs, turn, 0, unroll=9)
    acc_ref[...] = jnp.zeros_like(acc_ref)

    def turned(j, kind):
        part = arrived_ref[j * together : (j + 1) * together, kind * CAP : (kind + 1) * CAP, :]
        return jnp.transpose(part.reshape(WIDE, LANES).astype(f32))[:ROWS]

    own = jnp.concatenate([leaf_ref[...].astype(f32), jnp.zeros((ROWS - coeffs, boxes), f32)], 0)
    source_ref[...] = jnp.concatenate([own] + [turned(j, 0) for j in range(groups)], 0).astype(bf16)
    parent_ref[...] = jnp.concatenate(
        [turned(j, kind) for j in range(groups) for kind in (1, 2)], 0
    ).astype(bf16)
    lane_group = lax.broadcasted_iota(jnp.int32, (1, WIDE), 1) // (WIDE // STEP)
    mine = [jnp.where(lane_group == i, 1.0, 0.0).astype(bf16) for i in range(STEP)]
    fill = jnp.zeros((LANES - ROWS, WIDE), f32)

    def step(s, carry):
        row = clists_ref[s]
        rows = lists_ref[pl.ds(pl.multiple_of(s * STEP, STEP), STEP), :]
        found = jnp.dot(parent_ref[...], one_hot(row % WIDE, WIDE), preferred_element_type=f32)
        high = pick_block(found, row // WIDE, 0, 2 * ROWS, groups)
        low = pick_block(found, row // WIDE, ROWS, 2 * ROWS, groups)
        low = jnp.concatenate([low[:, LANES:], low[:, :LANES]], 1)
        high = jnp.concatenate([high, fill], 0).astype(bf16)
        low = jnp.concatenate([low, fill], 0).astype(bf16)
        matrix = []
        for i in range(STEP):
            offset = s * STEP + i
            row = rows[i : i + 1]
            found = jnp.dot(source_ref[...], one_hot(row % WIDE, WIDE), preferred_element_type=f32)
            column = pick_block(found, row // WIDE, 0, ROWS, groups + 1)
            column_ref[LANES * i : LANES * (i + 1), :WIDE] = jnp.concatenate([column, fill], 0).astype(bf16)
            column_ref[LANES * i : LANES * (i + 1), WIDE:] = (
                high * mine[i] + low * mine[(i + STEP // 2) % STEP]
            )
            start = pl.multiple_of(jnp.minimum(offset, offsets - 1) * ROWS, ROWS)
            matrix.append(matrix_ref[pl.ds(start, ROWS), :].astype(bf16))
        matrix = jnp.concatenate(matrix, 1)
        acc_ref[...] += jnp.dot(matrix, column_ref[...], preferred_element_type=f32)
        return carry

    lax.fori_loop(0, clists_ref.shape[0], step, 0, unroll=2)
    coarse = acc_ref[:, WIDE : WIDE + LANES] + acc_ref[:, WIDE + LANES :]
    coarse = coarse + pltpu.roll(coarse, LANES // 2, 1)
    coarse = coarse + pltpu.roll(coarse, LANES // 4, 1)
    coarse_round = coarse.astype(bf16)
    box = lax.broadcasted_iota(jnp.int32, (LANES, boxes), 1)
    parent = lax.broadcasted_iota(jnp.int32, (LANES, boxes), 0)
    spread = jnp.dot(
        coarse_round, jnp.where(box // 8 == parent, 1.0, 0.0).astype(bf16), preferred_element_type=f32
    )[:coeffs]
    octant = lax.broadcasted_iota(jnp.int32, (1, boxes), 1) % 8
    total = acc_ref[:coeffs, :WIDE]
    for c in range(8):
        total = total + jnp.dot(
            down_ref[c], jnp.where(octant == c, spread, 0.0).astype(bf16), preferred_element_type=f32
        )
    out_ref[...] = total


def far_sum(leaf_multipoles, arrived, translate, shift_down, leaf_lists, coarse_lists):
    coeffs, boxes = leaf_multipoles.shape
    offsets, coarse = coarse_lists.shape
    assert boxes == WIDE and coarse * STEP == WIDE
    peers = arrived.shape[0]
    groups = peers * CAP // WIDE
    steps = -(-offsets // STEP)
    extra = ((0, steps * STEP - offsets), (0, 0))
    lists = jnp.pad(leaf_lists, extra, constant_values=boxes + peers * CAP)
    clists = jnp.pad(coarse_lists, extra, constant_values=peers * coarse).reshape(steps, 1, WIDE)
    return pl.pallas_call(
        far_kernel,
        out_shape=jax.ShapeDtypeStruct((coeffs, boxes), f32),
        in_specs=[pl.BlockSpec(memory_space=pltpu.VMEM)] * 6,
        out_specs=pl.BlockSpec(memory_space=pltpu.VMEM),
        scratch_shapes=[
            pltpu.VMEM(((groups + 1) * ROWS, WIDE), bf16),
            pltpu.VMEM((groups * 2 * ROWS, WIDE), bf16),
            pltpu.VMEM((offsets * ROWS, LANES), f32),
            pltpu.VMEM((STEP * LANES, 2 * WIDE), bf16),
            pltpu.VMEM((ROWS, 2 * WIDE), f32),
        ],
        compiler_params=pltpu.CompilerParams(vmem_limit_bytes=40 * 2**20),
        name="far",
    )(leaf_multipoles, arrived, translate.transpose(1, 2, 0), shift_down, lists, clists)


def near_kernel(atoms_ref, edges_ref, lists_ref, counts_ref, out_ref):
    slots, boxes = out_ref.shape
    tiles = boxes // LANES

    def tile_sum(t):
        lanes = slice(t * LANES, (t + 1) * LANES)
        target = [atoms_ref[k * slots : (k + 1) * slots, lanes] for k in range(3)]

        def step(n, total):
            entry = lists_ref[n, :, lanes]
            local = entry - HALO
            inside = jnp.broadcast_to(local // LANES == t, (8, LANES)) & jnp.broadcast_to(local >= 0, (8, LANES))
            first = jnp.broadcast_to(local & (LANES - 1), (8, LANES))
            second = jnp.broadcast_to(local & (2 * HALO - 1), (8, LANES))
            source = []
            for r in range(4 * slots // 8):
                rows = slice(8 * r, 8 * (r + 1))
                one = jnp.take_along_axis(atoms_ref[rows, lanes], first, axis=1)
                two = jnp.take_along_axis(edges_ref[rows, lanes], second, axis=1)
                source.append(jnp.where(inside, one, two))
            source = jnp.concatenate(source, 0)
            present = entry < boxes + 2 * HALO
            charge = jnp.where(present, source[3 * slots :], 0.0)
            for b in range(slots):
                square = jnp.full((slots, LANES), softening, f32)
                for k in range(3):
                    diff = target[k] - source[k * slots + b : k * slots + b + 1]
                    square = square + diff * diff
                total = total + charge[b : b + 1] * lax.rsqrt(square)
            return total

        return lax.fori_loop(0, lists_ref.shape[0], step, jnp.zeros((slots, LANES), f32))

    slot = lax.broadcasted_iota(jnp.int32, (slots, LANES), 0)
    for t in range(tiles):
        lanes = slice(t * LANES, (t + 1) * LANES)
        out_ref[:, lanes] = jnp.where(slot < counts_ref[:, lanes], tile_sum(t), 0.0)


def near_part(positions, charges, counts, near_lists):
    boxes = counts.shape[0]
    slots = charges.shape[0] // boxes
    valid = jnp.arange(slots, dtype=jnp.int32)[:, None] < counts[None, :]
    charge = jnp.where(valid, charges.reshape(boxes, slots).T, 0.0)
    place = positions.reshape(3, boxes, slots).transpose(0, 2, 1).reshape(3 * slots, boxes)
    atoms = jnp.concatenate([place, charge], 0)
    count = lax.axis_size(DEVICES)
    forward = [(i, i + 1) for i in range(count - 1)]
    backward = [(target, source) for source, target in forward]
    below = lax.ppermute(atoms[:, boxes - HALO :], DEVICES, forward)
    above = lax.ppermute(atoms[:, :HALO], DEVICES, backward)
    fill = jnp.zeros((4 * slots, LANES - 2 * HALO), f32)
    edges = []
    for t in range(boxes // LANES):
        low, high = t * LANES, (t + 1) * LANES
        edges += [
            atoms[:, high : high + HALO] if high < boxes else above,
            atoms[:, low - HALO : low] if t else below,
            fill,
        ]
    potential = pl.pallas_call(
        near_kernel,
        out_shape=jax.ShapeDtypeStruct((slots, boxes), f32),
        in_specs=[pl.BlockSpec(memory_space=pltpu.VMEM)] * 4,
        out_specs=pl.BlockSpec(memory_space=pltpu.VMEM),
        name="near",
        cost_estimate=pl.CostEstimate(flops=40_000_000, bytes_accessed=2**18, transcendentals=0),
    )(atoms, jnp.concatenate(edges, 1), near_lists[:, None, :], counts[None, :])
    return potential.T.reshape(boxes * slots)


def far_part(leaf_multipoles, translate, shift_up, shift_down, export_rows, leaf_lists, coarse_lists):
    coeffs, boxes = leaf_multipoles.shape
    peers = export_rows.shape[1]
    exported = leaf_multipoles[:, export_rows[0].reshape(-1)].T.reshape(peers, CAP, coeffs)
    children = leaf_multipoles.reshape(coeffs, boxes // 8, 8)
    parents = jnp.einsum("ckm,mpc->pk", shift_up, children, preferred_element_type=f32)
    high = lax.reduce_precision(parents, 8, 7)
    both = jnp.concatenate([high, parents - high], 0).astype(bf16)
    outgoing = jnp.concatenate(
        [exported, jnp.broadcast_to(both[None], (peers,) + both.shape)], 1
    )
    outgoing = jnp.pad(outgoing, ((0, 0), (0, 0), (0, LANES - coeffs)))
    arrived = lax.all_to_all(outgoing, DEVICES, split_axis=0, concat_axis=0, tiled=True)
    return far_sum(leaf_multipoles, arrived, translate, shift_down, leaf_lists, coarse_lists)


def body(
    leaf_multipoles, translate, shift_up, shift_down, export_rows, leaf_lists, coarse_lists,
    positions, charges, counts, near_lists,
):
    local_field = far_part(
        leaf_multipoles, translate, shift_up, shift_down, export_rows, leaf_lists, coarse_lists
    )
    near_potential = near_part(positions, charges, counts, near_lists)
    return (local_field, near_potential)


def solution(mesh):
    every = ("rep",) + DEVICES
    in_specs = (
        P(None, every), P(), P(), P(), P(every, None, None), P(None, every), P(None, every),
        P(None, every), P(every), P(every), P(None, every),
    )
    out_specs = (P(None, every), P(every))
    return jax.shard_map(body, mesh=mesh, in_specs=in_specs, out_specs=out_specs, check_vma=False)
```

```python
import jax
import jax.numpy as jnp
from jax import lax
from jax.experimental import pallas as pl
from jax.experimental.pallas import tpu as pltpu
from jax.sharding import PartitionSpec as P

HALO = 16
CAP = 32
LANES = 128
WIDE = 256
ROWS = 88
STEP = 8

softening = 0.01
DEVICES = ("dom", "slab", "half")
f32 = jnp.float32
bf16 = jnp.bfloat16


def one_hot(row, width):
    numbers = lax.broadcasted_iota(jnp.int32, (width, row.shape[1]), 0).astype(f32).astype(bf16)
    picks = numbers == row.astype(f32).astype(bf16)
    return jnp.where(picks, jnp.ones((), bf16), jnp.zeros((), bf16))


def pick_block(stacked, block, first, stride, count):
    value = jnp.zeros((ROWS, stacked.shape[1]), f32)
    for j in range(count):
        start = first + j * stride
        value = jnp.where(block == j, stacked[start : start + ROWS], value)
    return value


def far_kernel(
    source_ref, parent_ref, translate_ref, down_ref, lists_ref, clists_ref, out_ref,
    page_ref, matrix_ref, column_ref, acc_ref, page_sem,
):
    coeffs, boxes = out_ref.shape
    offsets = translate_ref.shape[2]
    pieces = page_sem.shape[0]
    pages = coeffs // pieces
    groups = source_ref.shape[0] // ROWS - 1

    def fetch(j):
        part = pl.ds(j * pages, pages)
        return pltpu.make_async_copy(translate_ref.at[part], page_ref.at[part], page_sem.at[j])

    for j in range(pieces):
        fetch(j).start()
    acc_ref[...] = jnp.zeros_like(acc_ref)

    def turn(j, carry):
        fetch(j).wait()
        for i in range(pages):
            k = j * pages + i
            rows = jnp.concatenate(
                [page_ref[k].astype(f32), jnp.zeros((LANES - coeffs, offsets), f32)], 0
            )
            matrix_ref[pl.ds(k, offsets, stride=ROWS), :] = jnp.transpose(rows)
        return carry

    lax.fori_loop(0, pieces, turn, 0)
    lane_group = lax.broadcasted_iota(jnp.int32, (1, WIDE), 1) // (WIDE // STEP)
    mine = [jnp.where(lane_group == i, 1.0, 0.0).astype(bf16) for i in range(STEP)]
    fill = jnp.zeros((LANES - ROWS, WIDE), f32)

    def step(s, carry):
        row = clists_ref[s]
        rows = lists_ref[pl.ds(pl.multiple_of(s * STEP, STEP), STEP), :]
        found = jnp.dot(parent_ref[...], one_hot(row % WIDE, WIDE), preferred_element_type=f32)
        high = pick_block(found, row // WIDE, 0, 2 * ROWS, groups)
        low = pick_block(found, row // WIDE, ROWS, 2 * ROWS, groups)
        low = jnp.concatenate([low[:, LANES:], low[:, :LANES]], 1)
        high = jnp.concatenate([high, fill], 0).astype(bf16)
        low = jnp.concatenate([low, fill], 0).astype(bf16)
        matrix = []
        for i in range(STEP):
            offset = s * STEP + i
            row = rows[i : i + 1]
            found = jnp.dot(source_ref[...], one_hot(row % WIDE, WIDE), preferred_element_type=f32)
            column = pick_block(found, row // WIDE, 0, ROWS, groups + 1)
            column_ref[LANES * i : LANES * (i + 1), :WIDE] = jnp.concatenate([column, fill], 0).astype(bf16)
            column_ref[LANES * i : LANES * (i + 1), WIDE:] = (
                high * mine[i] + low * mine[(i + STEP // 2) % STEP]
            )
            start = pl.multiple_of(jnp.minimum(offset, offsets - 1) * ROWS, ROWS)
            matrix.append(matrix_ref[pl.ds(start, ROWS), :].astype(bf16))
        matrix = jnp.concatenate(matrix, 1)
        acc_ref[...] += jnp.dot(matrix, column_ref[...], preferred_element_type=f32)
        return carry

    lax.fori_loop(0, clists_ref.shape[0], step, 0, unroll=2)
    coarse = acc_ref[:, WIDE : WIDE + LANES] + acc_ref[:, WIDE + LANES :]
    coarse = coarse + pltpu.roll(coarse, LANES // 2, 1)
    coarse = coarse + pltpu.roll(coarse, LANES // 4, 1)
    coarse_round = coarse.astype(bf16)
    box = lax.broadcasted_iota(jnp.int32, (LANES, boxes), 1)
    parent = lax.broadcasted_iota(jnp.int32, (LANES, boxes), 0)
    spread = jnp.dot(
        coarse_round, jnp.where(box // 8 == parent, 1.0, 0.0).astype(bf16), preferred_element_type=f32
    )[:coeffs]
    octant = lax.broadcasted_iota(jnp.int32, (1, boxes), 1) % 8
    total = acc_ref[:coeffs, :WIDE]
    for c in range(8):
        total = total + jnp.dot(
            down_ref[c], jnp.where(octant == c, spread, 0.0).astype(bf16), preferred_element_type=f32
        )
    out_ref[...] = total


def far_sum(source, parents, translate, shift_down, leaf_lists, coarse_lists):
    offsets, boxes = leaf_lists.shape
    coeffs = translate.shape[1]
    coarse = coarse_lists.shape[1]
    assert boxes == WIDE and coarse * STEP == WIDE
    groups = source.shape[0] // ROWS - 1
    steps = -(-offsets // STEP)
    extra = ((0, steps * STEP - offsets), (0, 0))
    lists = jnp.pad(leaf_lists, extra, constant_values=(groups + 1) * WIDE)
    clists = jnp.pad(coarse_lists, extra, constant_values=groups * WIDE).reshape(steps, 1, WIDE)
    vmem = pl.BlockSpec(memory_space=pltpu.VMEM)
    return pl.pallas_call(
        far_kernel,
        out_shape=jax.ShapeDtypeStruct((coeffs, boxes), f32),
        in_specs=[vmem, vmem, pl.BlockSpec(memory_space=pl.ANY), vmem, vmem, vmem],
        out_specs=vmem,
        scratch_shapes=[
            pltpu.VMEM((coeffs, coeffs, offsets), bf16),
            pltpu.VMEM((offsets * ROWS, LANES), f32),
            pltpu.VMEM((STEP * LANES, 2 * WIDE), bf16),
            pltpu.VMEM((ROWS, 2 * WIDE), f32),
            pltpu.SemaphoreType.DMA((9 if coeffs % 9 == 0 else 1,)),
        ],
        compiler_params=pltpu.CompilerParams(vmem_limit_bytes=48 * 2**20),
        name="far",
    )(source, parents, translate.transpose(1, 2, 0), shift_down, lists, clists)


def exchange_kernel(
    leaf_ref, rows_ref, up_ref, atoms_ref, lists_ref, counts_ref,
    source_ref, parent_ref, near_ref,
    send_ref, land_ref, edge_ref, side_ref, send_sem, land_sem, edge_send_sem, edge_land_sem,
):
    coeffs, boxes = leaf_ref.shape
    slots = near_ref.shape[0]
    peers = send_ref.shape[0]
    tiles = boxes // LANES
    sizes = [lax.axis_size(axis) for axis in DEVICES]
    dom, slab, half = [lax.axis_index(axis) for axis in DEVICES]
    me = (dom * sizes[1] + slab) * sizes[2] + half

    def place(index):
        return {
            "dom": index // (sizes[1] * sizes[2]),
            "slab": (index // sizes[2]) % sizes[1],
            "half": index % sizes[2],
        }

    barrier = pltpu.get_barrier_semaphore()

    def greet(d, carry):
        pl.semaphore_signal(
            barrier, inc=1, device_id=place((me + d) % peers), device_id_type=pl.DeviceIdType.MESH
        )
        return carry

    lax.fori_loop(1, peers, greet, 0)

    own = jnp.concatenate([leaf_ref[...].astype(f32), jnp.zeros((LANES - coeffs, boxes), f32)], 0)
    packed = own.astype(bf16)
    up = up_ref[...]
    high = up.astype(bf16)
    low = (up - high.astype(f32)).astype(bf16)
    together = WIDE // CAP
    for j in range(peers // together):
        hot = one_hot(rows_ref[:, j * WIDE : (j + 1) * WIDE], boxes)
        part = jnp.transpose(jnp.dot(packed, hot, preferred_element_type=f32)).astype(bf16)
        for i in range(together):
            p = j * together + i
            send_ref[p, :CAP, :] = part[i * CAP : (i + 1) * CAP]
            send_ref[p, CAP : 2 * CAP, :] = high
            send_ref[p, 2 * CAP :, :] = low
    pl.semaphore_wait(barrier, peers - 1)

    def edge(side):
        lanes = pl.ds((1 - side) * (boxes - LANES), LANES)
        return pltpu.make_async_remote_copy(
            src_ref=atoms_ref.at[:, lanes], dst_ref=edge_ref.at[side],
            send_sem=edge_send_sem.at[side], recv_sem=edge_land_sem.at[side],
            device_id=place((me + 1 - 2 * side + peers) % peers),
            device_id_type=pl.DeviceIdType.MESH,
        )

    def sending(d):
        return pltpu.make_async_remote_copy(
            src_ref=send_ref.at[(me + d) % peers], dst_ref=land_ref.at[me],
            send_sem=send_sem.at[d], recv_sem=land_sem.at[d],
            device_id=place((me + d) % peers), device_id_type=pl.DeviceIdType.MESH,
        )

    def landing(d):
        sender = (me - d + peers) % peers
        return pltpu.make_async_remote_copy(
            src_ref=send_ref.at[sender], dst_ref=land_ref.at[sender],
            send_sem=send_sem.at[d], recv_sem=land_sem.at[d],
            device_id=place(sender), device_id_type=pl.DeviceIdType.MESH,
        )

    for side in range(2):
        edge(side).start()

    def start(d, carry):
        sending(d).start()
        return carry

    lax.fori_loop(1, peers, start, 0)
    land_ref[me] = send_ref[me]

    for side in range(2):
        edge(side).wait()
    below = jnp.where(me > 0, edge_ref[0], 0.0)
    above = jnp.where(me < peers - 1, edge_ref[1], 0.0)
    lower = lax.broadcasted_iota(jnp.int32, (1, LANES), 1) < LANES // 2
    for t in range(tiles):
        after = atoms_ref[:, (t + 1) * LANES : (t + 2) * LANES] if t + 1 < tiles else above
        before = atoms_ref[:, (t - 1) * LANES : t * LANES] if t else below
        side_ref[:, t * LANES : (t + 1) * LANES] = jnp.where(lower, after, before)

    def step(n, totals):
        out = []
        for t in range(tiles):
            lanes = slice(t * LANES, (t + 1) * LANES)
            total = totals[t]
            entry = lists_ref[n, :, lanes]
            local = jnp.broadcast_to(entry - HALO, (8, LANES))
            inside = (local >= t * LANES) & (local < (t + 1) * LANES)
            lane = local & (LANES - 1)
            source = []
            for r in range(4 * slots // 8):
                rows = slice(8 * r, 8 * (r + 1))
                one = jnp.take_along_axis(atoms_ref[rows, lanes], lane, axis=1)
                two = jnp.take_along_axis(side_ref[rows, lanes], lane, axis=1)
                source.append(jnp.where(inside, one, two))
            source = jnp.concatenate(source, 0)
            charge = jnp.where(entry < boxes + 2 * HALO, source[3 * slots :], 0.0)
            target = [atoms_ref[k * slots : (k + 1) * slots, lanes] for k in range(3)]
            for b in range(slots):
                square = jnp.full((slots, LANES), softening, f32)
                for k in range(3):
                    diff = target[k] - source[k * slots + b : k * slots + b + 1]
                    square = square + diff * diff
                total = total + charge[b : b + 1] * lax.rsqrt(square)
            out.append(total)
        return tuple(out)

    zero = jnp.zeros((slots, LANES), f32)
    totals = lax.fori_loop(0, lists_ref.shape[0], step, (zero,) * tiles)
    slot = lax.broadcasted_iota(jnp.int32, (slots, LANES), 0)
    for t in range(tiles):
        lanes = slice(t * LANES, (t + 1) * LANES)
        near_ref[:, lanes] = jnp.where(slot < counts_ref[:, lanes], totals[t], 0.0)

    def finish(d, carry):
        sending(d).wait_send()
        landing(d).wait_recv()
        return carry

    lax.fori_loop(1, peers, finish, 0)

    def turned(j, kind):
        part = land_ref[j * together : (j + 1) * together, kind * CAP : (kind + 1) * CAP, :]
        return jnp.transpose(part.reshape(WIDE, LANES).astype(f32))[:ROWS]

    groups = peers // together
    source_ref[...] = jnp.concatenate(
        [own[:ROWS]] + [turned(j, 0) for j in range(groups)], 0
    ).astype(bf16)
    parent_ref[...] = jnp.concatenate(
        [turned(j, kind) for j in range(groups) for kind in (1, 2)], 0
    ).astype(bf16)


def exchange(leaf_multipoles, shift_up, export_rows, positions, charges, counts, near_lists):
    coeffs, boxes = leaf_multipoles.shape
    peers = export_rows.shape[1]
    slots = charges.shape[0] // boxes
    groups = peers * CAP // WIDE
    assert boxes // 8 == CAP
    children = leaf_multipoles.reshape(coeffs, boxes // 8, 8)
    parents = jnp.einsum("ckm,mpc->pk", shift_up, children, preferred_element_type=f32)
    parents = jnp.pad(parents, ((0, 0), (0, LANES - coeffs)))
    valid = jnp.arange(slots, dtype=jnp.int32)[:, None] < counts[None, :]
    charge = jnp.where(valid, charges.reshape(boxes, slots).T, 0.0)
    place = positions.reshape(3, boxes, slots).transpose(0, 2, 1).reshape(3 * slots, boxes)
    atoms = jnp.concatenate([place, charge], 0)
    vmem = pl.BlockSpec(memory_space=pltpu.VMEM)
    source, parent, potential = pl.pallas_call(
        exchange_kernel,
        out_shape=(
            jax.ShapeDtypeStruct(((groups + 1) * ROWS, WIDE), bf16),
            jax.ShapeDtypeStruct((groups * 2 * ROWS, WIDE), bf16),
            jax.ShapeDtypeStruct((slots, boxes), f32),
        ),
        in_specs=[vmem] * 6,
        out_specs=(vmem,) * 3,
        scratch_shapes=[
            pltpu.VMEM((peers, 3 * CAP, LANES), bf16),
            pltpu.VMEM((peers, 3 * CAP, LANES), bf16),
            pltpu.VMEM((2, 4 * slots, LANES), f32),
            pltpu.VMEM((4 * slots, boxes), f32),
            pltpu.SemaphoreType.DMA((peers,)),
            pltpu.SemaphoreType.DMA((peers,)),
            pltpu.SemaphoreType.DMA((2,)),
            pltpu.SemaphoreType.DMA((2,)),
        ],
        compiler_params=pltpu.CompilerParams(
            collective_id=0, has_side_effects=True, vmem_limit_bytes=32 * 2**20
        ),
        name="exchange",
    )(
        leaf_multipoles, export_rows.reshape(1, peers * CAP), parents, atoms,
        near_lists[:, None, :], counts[None, :],
    )
    return source, parent, potential.T.reshape(boxes * slots)


def body(
    leaf_multipoles, translate, shift_up, shift_down, export_rows, leaf_lists, coarse_lists,
    positions, charges, counts, near_lists,
):
    source, parents, near_potential = exchange(
        leaf_multipoles, shift_up, export_rows, positions, charges, counts, near_lists
    )
    local_field = far_sum(source, parents, translate, shift_down, leaf_lists, coarse_lists)
    return (local_field, near_potential)


def solution(mesh):
    every = ("rep",) + DEVICES
    in_specs = (
        P(None, every), P(), P(), P(), P(every, None, None), P(None, every), P(None, every),
        P(None, every), P(every), P(every), P(None, every),
    )
    out_specs = (P(None, every), P(every))
    return jax.shard_map(body, mesh=mesh, in_specs=in_specs, out_specs=out_specs, check_vma=False)
```

```python
import jax
import jax.numpy as jnp
from jax import lax
from jax.experimental import pallas as pl
from jax.experimental.pallas import tpu as pltpu
from jax.sharding import PartitionSpec as P

HALO = 16
CAP = 32
LANES = 128
WIDE = 256
ROWS = 88
STEP = 8

softening = 0.01
DEVICES = ("dom", "slab", "half")
f32 = jnp.float32
bf16 = jnp.bfloat16


def one_hot(row, width):
    numbers = lax.broadcasted_iota(jnp.int32, (width, row.shape[1]), 0).astype(f32).astype(bf16)
    picks = numbers == row.astype(f32).astype(bf16)
    return jnp.where(picks, jnp.ones((), bf16), jnp.zeros((), bf16))


def pick_block(stacked, block, first, stride, count):
    value = jnp.zeros((ROWS, stacked.shape[1]), f32)
    for j in range(count):
        start = first + j * stride
        value = jnp.where(block == j, stacked[start : start + ROWS], value)
    return value


def unroll_of(count):
    return next(k for k in (3, 2, 1) if count % k == 0)


def far_kernel(
    source_ref, parent_ref, translate_ref, down_ref, lists_ref, clists_ref, out_ref,
    page_ref, matrix_ref, column_ref, acc_ref, page_sem,
):
    coeffs, boxes = out_ref.shape
    offsets = translate_ref.shape[2]
    pieces = page_sem.shape[0]
    pages = coeffs // pieces
    groups = source_ref.shape[0] // ROWS - 1

    def fetch(j):
        part = pl.ds(j * pages, pages)
        return pltpu.make_async_copy(translate_ref.at[part], page_ref.at[part], page_sem.at[j])

    for j in range(pieces):
        fetch(j).start()
    acc_ref[...] = jnp.zeros_like(acc_ref)

    def turn(j, carry):
        fetch(j).wait()
        for i in range(pages):
            k = j * pages + i
            rows = jnp.concatenate(
                [page_ref[k].astype(f32), jnp.zeros((LANES - coeffs, offsets), f32)], 0
            )
            matrix_ref[pl.ds(k, offsets, stride=ROWS), :] = jnp.transpose(rows)
        return carry

    lax.fori_loop(0, pieces, turn, 0)
    lane_group = lax.broadcasted_iota(jnp.int32, (1, WIDE), 1) // (WIDE // STEP)
    mine = [jnp.where(lane_group == i, 1.0, 0.0).astype(bf16) for i in range(STEP)]
    fill = jnp.zeros((LANES - ROWS, WIDE), f32)

    def some(s, rows):
        count = rows.shape[0]
        row = clists_ref[s]
        found = jnp.dot(parent_ref[...], one_hot(row % WIDE, WIDE), preferred_element_type=f32)
        high = pick_block(found, row // WIDE, 0, 2 * ROWS, groups)
        low = pick_block(found, row // WIDE, ROWS, 2 * ROWS, groups)
        low = jnp.concatenate([low[:, LANES:], low[:, :LANES]], 1)
        high = jnp.concatenate([high, fill], 0).astype(bf16)
        low = jnp.concatenate([low, fill], 0).astype(bf16)
        matrix = []
        for i in range(count):
            offset = s * STEP + i
            row = rows[i : i + 1]
            found = jnp.dot(source_ref[...], one_hot(row % WIDE, WIDE), preferred_element_type=f32)
            column = pick_block(found, row // WIDE, 0, ROWS, groups + 1)
            column_ref[LANES * i : LANES * (i + 1), :WIDE] = jnp.concatenate([column, fill], 0).astype(bf16)
            column_ref[LANES * i : LANES * (i + 1), WIDE:] = (
                high * mine[i] + low * mine[(i + STEP // 2) % STEP]
            )
            start = pl.multiple_of(offset * ROWS, ROWS)
            matrix.append(matrix_ref[pl.ds(start, ROWS), :].astype(bf16))
        matrix = jnp.concatenate(matrix, 1)
        acc_ref[...] += jnp.dot(
            matrix, column_ref[: LANES * count], preferred_element_type=f32
        )

    def step(s, carry):
        some(s, lists_ref[pl.ds(pl.multiple_of(s * STEP, STEP), STEP), :])
        return carry

    full = offsets // STEP
    lax.fori_loop(0, full, step, 0, unroll=unroll_of(full))
    if full * STEP < offsets:
        some(full, lists_ref[full * STEP :, :])
    coarse = acc_ref[:, WIDE : WIDE + LANES] + acc_ref[:, WIDE + LANES :]
    coarse = coarse + pltpu.roll(coarse, LANES // 2, 1)
    coarse = coarse + pltpu.roll(coarse, LANES // 4, 1)
    coarse_round = coarse.astype(bf16)
    box = lax.broadcasted_iota(jnp.int32, (LANES, boxes), 1)
    parent = lax.broadcasted_iota(jnp.int32, (LANES, boxes), 0)
    spread = jnp.dot(
        coarse_round, jnp.where(box // 8 == parent, 1.0, 0.0).astype(bf16), preferred_element_type=f32
    )[:coeffs]
    octant = lax.broadcasted_iota(jnp.int32, (1, boxes), 1) % 8
    total = acc_ref[:coeffs, :WIDE]
    for c in range(8):
        total = total + jnp.dot(
            down_ref[c], jnp.where(octant == c, spread, 0.0).astype(bf16), preferred_element_type=f32
        )
    out_ref[...] = total


def far_sum(source, parents, translate, shift_down, leaf_lists, coarse_lists):
    offsets, boxes = leaf_lists.shape
    coeffs = translate.shape[1]
    coarse = coarse_lists.shape[1]
    assert boxes == WIDE and coarse * STEP == WIDE
    groups = source.shape[0] // ROWS - 1
    steps = -(-offsets // STEP)
    extra = ((0, steps * STEP - offsets), (0, 0))
    clists = jnp.pad(coarse_lists, extra, constant_values=groups * WIDE).reshape(steps, 1, WIDE)
    vmem = pl.BlockSpec(memory_space=pltpu.VMEM)
    return pl.pallas_call(
        far_kernel,
        out_shape=jax.ShapeDtypeStruct((coeffs, boxes), f32),
        in_specs=[vmem, vmem, pl.BlockSpec(memory_space=pl.ANY), vmem, vmem, vmem],
        out_specs=vmem,
        scratch_shapes=[
            pltpu.VMEM((coeffs, coeffs, offsets), bf16),
            pltpu.VMEM((offsets * ROWS, LANES), f32),
            pltpu.VMEM((STEP * LANES, 2 * WIDE), bf16),
            pltpu.VMEM((ROWS, 2 * WIDE), f32),
            pltpu.SemaphoreType.DMA((9 if coeffs % 9 == 0 else 1,)),
        ],
        compiler_params=pltpu.CompilerParams(vmem_limit_bytes=48 * 2**20),
        name="far",
    )(source, parents, translate.transpose(1, 2, 0), shift_down, leaf_lists, clists)


def exchange_kernel(
    leaf_ref, rows_ref, up_ref, atoms_ref, lists_ref, counts_ref,
    source_ref, parent_ref, near_ref,
    send_ref, land_ref, edge_ref, side_ref, entry_ref, send_sem, land_sem, edge_send_sem, edge_land_sem,
):
    coeffs, boxes = leaf_ref.shape
    slots = near_ref.shape[0]
    peers = send_ref.shape[0]
    tiles = boxes // LANES
    sizes = [lax.axis_size(axis) for axis in DEVICES]
    dom, slab, half = [lax.axis_index(axis) for axis in DEVICES]
    me = (dom * sizes[1] + slab) * sizes[2] + half

    def place(index):
        return {
            "dom": index // (sizes[1] * sizes[2]),
            "slab": (index // sizes[2]) % sizes[1],
            "half": index % sizes[2],
        }

    barrier = pltpu.get_barrier_semaphore()

    def greet(d, carry):
        pl.semaphore_signal(
            barrier, inc=1, device_id=place((me + d) % peers), device_id_type=pl.DeviceIdType.MESH
        )
        return carry

    lax.fori_loop(1, peers, greet, 0)

    own = jnp.concatenate([leaf_ref[...].astype(f32), jnp.zeros((LANES - coeffs, boxes), f32)], 0)
    packed = own.astype(bf16)
    up = up_ref[...]
    high = up.astype(bf16)
    low = (up - high.astype(f32)).astype(bf16)
    together = WIDE // CAP
    for j in range(peers // together):
        named = [rows_ref[p : p + 1, :] for p in range(j * together, (j + 1) * together)]
        hot = one_hot(jnp.concatenate(named, 1), boxes)
        part = jnp.transpose(jnp.dot(packed, hot, preferred_element_type=f32)).astype(bf16)
        for i in range(together):
            p = j * together + i
            send_ref[p, :CAP, :] = part[i * CAP : (i + 1) * CAP]
            send_ref[p, CAP : 2 * CAP, :] = high
            send_ref[p, 2 * CAP :, :] = low
    pl.semaphore_wait(barrier, peers - 1)

    def edge(side):
        lanes = pl.ds((1 - side) * (boxes - LANES), LANES)
        return pltpu.make_async_remote_copy(
            src_ref=atoms_ref.at[:, lanes], dst_ref=edge_ref.at[side],
            send_sem=edge_send_sem.at[side], recv_sem=edge_land_sem.at[side],
            device_id=place((me + 1 - 2 * side + peers) % peers),
            device_id_type=pl.DeviceIdType.MESH,
        )

    def sending(d):
        return pltpu.make_async_remote_copy(
            src_ref=send_ref.at[(me + d) % peers], dst_ref=land_ref.at[me],
            send_sem=send_sem.at[d], recv_sem=land_sem.at[d],
            device_id=place((me + d) % peers), device_id_type=pl.DeviceIdType.MESH,
        )

    def landing(d):
        sender = (me - d + peers) % peers
        return pltpu.make_async_remote_copy(
            src_ref=send_ref.at[sender], dst_ref=land_ref.at[sender],
            send_sem=send_sem.at[d], recv_sem=land_sem.at[d],
            device_id=place(sender), device_id_type=pl.DeviceIdType.MESH,
        )

    for side in range(2):
        edge(side).start()

    def start(d, carry):
        sending(d).start()
        return carry

    lax.fori_loop(1, peers, start, 0)
    land_ref[me] = send_ref[me]

    for side in range(2):
        edge(side).wait()
    below = jnp.where(me > 0, edge_ref[0], 0.0)
    above = jnp.where(me < peers - 1, edge_ref[1], 0.0)
    lower = lax.broadcasted_iota(jnp.int32, (1, LANES), 1) < LANES // 2
    for t in range(tiles):
        after = atoms_ref[:, (t + 1) * LANES : (t + 2) * LANES] if t + 1 < tiles else above
        before = atoms_ref[:, (t - 1) * LANES : t * LANES] if t else below
        side_ref[:, t * LANES : (t + 1) * LANES] = jnp.where(lower, after, before)

    for n in range(lists_ref.shape[0]):
        entry_ref[n] = lists_ref[n : n + 1, :]

    def step(n, totals):
        out = []
        for t in range(tiles):
            lanes = slice(t * LANES, (t + 1) * LANES)
            total = totals[t]
            entry = entry_ref[n, :, lanes]
            local = jnp.broadcast_to(entry - HALO, (8, LANES))
            inside = (local >= t * LANES) & (local < (t + 1) * LANES)
            lane = local & (LANES - 1)
            source = []
            for r in range(4 * slots // 8):
                rows = slice(8 * r, 8 * (r + 1))
                one = jnp.take_along_axis(atoms_ref[rows, lanes], lane, axis=1)
                two = jnp.take_along_axis(side_ref[rows, lanes], lane, axis=1)
                source.append(jnp.where(inside, one, two))
            source = jnp.concatenate(source, 0)
            charge = jnp.where(entry < boxes + 2 * HALO, source[3 * slots :], 0.0)
            target = [atoms_ref[k * slots : (k + 1) * slots, lanes] for k in range(3)]
            for b in range(slots):
                square = jnp.full((slots, LANES), softening, f32)
                for k in range(3):
                    diff = target[k] - source[k * slots + b : k * slots + b + 1]
                    square = square + diff * diff
                total = total + charge[b : b + 1] * lax.rsqrt(square)
            out.append(total)
        return tuple(out)

    zero = jnp.zeros((slots, LANES), f32)
    totals = lax.fori_loop(
        0, lists_ref.shape[0], step, (zero,) * tiles, unroll=unroll_of(lists_ref.shape[0])
    )
    slot = lax.broadcasted_iota(jnp.int32, (slots, LANES), 0)
    for t in range(tiles):
        lanes = slice(t * LANES, (t + 1) * LANES)
        near_ref[:, lanes] = jnp.where(slot < counts_ref[:, lanes], totals[t], 0.0)

    def finish(d, carry):
        sending(d).wait_send()
        landing(d).wait_recv()
        return carry

    lax.fori_loop(1, peers, finish, 0)

    def turned(j, kind):
        part = land_ref[j * together : (j + 1) * together, kind * CAP : (kind + 1) * CAP, :]
        return jnp.transpose(part.reshape(WIDE, LANES).astype(f32))[:ROWS]

    groups = peers // together
    source_ref[...] = jnp.concatenate(
        [own[:ROWS]] + [turned(j, 0) for j in range(groups)], 0
    ).astype(bf16)
    parent_ref[...] = jnp.concatenate(
        [turned(j, kind) for j in range(groups) for kind in (1, 2)], 0
    ).astype(bf16)


def exchange(leaf_multipoles, shift_up, export_rows, positions, charges, counts, near_lists):
    coeffs, boxes = leaf_multipoles.shape
    peers = export_rows.shape[1]
    slots = charges.shape[0] // boxes
    groups = peers * CAP // WIDE
    assert boxes // 8 == CAP
    children = leaf_multipoles.reshape(coeffs, boxes // 8, 8)
    parents = jnp.einsum("ckm,mpc->pk", shift_up, children, preferred_element_type=f32)
    parents = jnp.pad(parents, ((0, 0), (0, LANES - coeffs)))
    valid = jnp.arange(slots, dtype=jnp.int32)[:, None] < counts[None, :]
    charge = jnp.where(valid, charges.reshape(boxes, slots).T, 0.0)
    place = positions.reshape(3, boxes, slots).transpose(0, 2, 1).reshape(3 * slots, boxes)
    atoms = jnp.concatenate([place, charge], 0)
    vmem = pl.BlockSpec(memory_space=pltpu.VMEM)
    source, parent, potential = pl.pallas_call(
        exchange_kernel,
        out_shape=(
            jax.ShapeDtypeStruct(((groups + 1) * ROWS, WIDE), bf16),
            jax.ShapeDtypeStruct((groups * 2 * ROWS, WIDE), bf16),
            jax.ShapeDtypeStruct((slots, boxes), f32),
        ),
        in_specs=[vmem] * 6,
        out_specs=(vmem,) * 3,
        scratch_shapes=[
            pltpu.VMEM((peers, 3 * CAP, LANES), bf16),
            pltpu.VMEM((peers, 3 * CAP, LANES), bf16),
            pltpu.VMEM((2, 4 * slots, LANES), f32),
            pltpu.VMEM((4 * slots, boxes), f32),
            pltpu.VMEM((near_lists.shape[0], 1, boxes), jnp.int32),
            pltpu.SemaphoreType.DMA((peers,)),
            pltpu.SemaphoreType.DMA((peers,)),
            pltpu.SemaphoreType.DMA((2,)),
            pltpu.SemaphoreType.DMA((2,)),
        ],
        compiler_params=pltpu.CompilerParams(
            collective_id=0, has_side_effects=True, vmem_limit_bytes=32 * 2**20
        ),
        name="exchange",
    )(
        leaf_multipoles, export_rows[0], parents, atoms,
        near_lists, counts[None, :],
    )
    return source, parent, potential.T.reshape(boxes * slots)


def body(
    leaf_multipoles, translate, shift_up, shift_down, export_rows, leaf_lists, coarse_lists,
    positions, charges, counts, near_lists,
):
    source, parents, near_potential = exchange(
        leaf_multipoles, shift_up, export_rows, positions, charges, counts, near_lists
    )
    local_field = far_sum(source, parents, translate, shift_down, leaf_lists, coarse_lists)
    return (local_field, near_potential)


def solution(mesh):
    every = ("rep",) + DEVICES
    in_specs = (
        P(None, every), P(), P(), P(), P(every, None, None), P(None, every), P(None, every),
        P(None, every), P(every), P(every), P(None, every),
    )
    out_specs = (P(None, every), P(every))
    return jax.shard_map(body, mesh=mesh, in_specs=in_specs, out_specs=out_specs, check_vma=False)
```

```python
import jax
import jax.numpy as jnp
from jax import lax
from jax.experimental import pallas as pl
from jax.experimental.pallas import tpu as pltpu
from jax.sharding import PartitionSpec as P

HALO = 16
CAP = 32
LANES = 128
WIDE = 256
ROWS = 88
KEPT = 96
STEP = 8

softening = 0.01
DEVICES = ("dom", "slab", "half")
f32 = jnp.float32
bf16 = jnp.bfloat16


def one_hot(row, width):
    numbers = lax.broadcasted_iota(jnp.int32, (width, row.shape[1]), 0).astype(f32).astype(bf16)
    picks = numbers == row.astype(f32).astype(bf16)
    return jnp.where(picks, jnp.ones((), bf16), jnp.zeros((), bf16))


def pick_block(stacked, block, first, stride, count):
    value = jnp.zeros((ROWS, stacked.shape[1]), f32)
    for j in range(count):
        start = first + j * stride
        value = jnp.where(block == j, stacked[start : start + ROWS], value)
    return value


def unroll_of(count):
    return next(k for k in (3, 2, 1) if count % k == 0)


def far_kernel(
    source_ref, parent_ref, translate_ref, down_ref, lists_ref, clists_ref, out_ref,
    page_ref, matrix_ref, column_ref, acc_ref, page_sem,
):
    coeffs, boxes = out_ref.shape
    offsets = translate_ref.shape[2]
    pieces = page_sem.shape[0]
    pages = coeffs // pieces
    groups = source_ref.shape[0] // ROWS - 1

    def fetch(j):
        part = pl.ds(j * pages, pages)
        return pltpu.make_async_copy(translate_ref.at[part], page_ref.at[part], page_sem.at[j])

    for j in range(pieces):
        fetch(j).start()
    acc_ref[...] = jnp.zeros_like(acc_ref)
    column_ref[...] = jnp.zeros_like(column_ref)

    def turn(j, carry):
        fetch(j).wait()
        for i in range(pages):
            k = j * pages + i
            rows = jnp.concatenate(
                [page_ref[k].astype(f32), jnp.zeros((LANES - coeffs, offsets), f32)], 0
            )
            matrix_ref[pl.ds(k, offsets, stride=ROWS), :] = jnp.transpose(rows)
        return carry

    lax.fori_loop(0, pieces, turn, 0)
    lane_group = lax.broadcasted_iota(jnp.int32, (1, WIDE), 1) // (WIDE // STEP)
    mine = [jnp.where(lane_group == i, 1.0, 0.0).astype(bf16) for i in range(STEP)]
    fill = jnp.zeros((KEPT - ROWS, WIDE), f32)

    def some(s, rows):
        count = rows.shape[0]
        row = clists_ref[s]
        found = jnp.dot(parent_ref[...], one_hot(row % WIDE, WIDE), preferred_element_type=f32)
        high = pick_block(found, row // WIDE, 0, 2 * ROWS, groups)
        low = pick_block(found, row // WIDE, ROWS, 2 * ROWS, groups)
        low = jnp.concatenate([low[:, LANES:], low[:, :LANES]], 1)
        high = jnp.concatenate([high, fill], 0).astype(bf16)
        low = jnp.concatenate([low, fill], 0).astype(bf16)
        matrix = []
        for i in range(count):
            offset = s * STEP + i
            row = rows[i : i + 1]
            found = jnp.dot(source_ref[...], one_hot(row % WIDE, WIDE), preferred_element_type=f32)
            column = pick_block(found, row // WIDE, 0, ROWS, groups + 1)
            column_ref[LANES * i : LANES * i + KEPT, :WIDE] = jnp.concatenate([column, fill], 0).astype(bf16)
            column_ref[LANES * i : LANES * i + KEPT, WIDE:] = (
                high * mine[i] + low * mine[(i + STEP // 2) % STEP]
            )
            start = pl.multiple_of(offset * ROWS, ROWS)
            matrix.append(matrix_ref[pl.ds(start, ROWS), :].astype(bf16))
        matrix = jnp.concatenate(matrix, 1)
        acc_ref[...] += jnp.dot(
            matrix, column_ref[: LANES * count], preferred_element_type=f32
        )

    def step(s, carry):
        some(s, lists_ref[pl.ds(pl.multiple_of(s * STEP, STEP), STEP), :])
        return carry

    full = offsets // STEP
    lax.fori_loop(0, full, step, 0, unroll=unroll_of(full))
    if full * STEP < offsets:
        some(full, lists_ref[full * STEP :, :])
    coarse = acc_ref[:, WIDE : WIDE + LANES] + acc_ref[:, WIDE + LANES :]
    coarse = coarse + pltpu.roll(coarse, LANES // 2, 1)
    coarse = coarse + pltpu.roll(coarse, LANES // 4, 1)
    coarse_round = coarse.astype(bf16)
    box = lax.broadcasted_iota(jnp.int32, (LANES, boxes), 1)
    parent = lax.broadcasted_iota(jnp.int32, (LANES, boxes), 0)
    spread = jnp.dot(
        coarse_round, jnp.where(box // 8 == parent, 1.0, 0.0).astype(bf16), preferred_element_type=f32
    )[:coeffs]
    octant = lax.broadcasted_iota(jnp.int32, (1, boxes), 1) % 8
    total = acc_ref[:coeffs, :WIDE]
    for c in range(8):
        total = total + jnp.dot(
            down_ref[c], jnp.where(octant == c, spread, 0.0).astype(bf16), preferred_element_type=f32
        )
    out_ref[...] = total


def far_sum(source, parents, translate, shift_down, leaf_lists, coarse_lists):
    offsets, boxes = leaf_lists.shape
    coeffs = translate.shape[1]
    coarse = coarse_lists.shape[1]
    assert boxes == WIDE and coarse * STEP == WIDE
    groups = source.shape[0] // ROWS - 1
    steps = -(-offsets // STEP)
    extra = ((0, steps * STEP - offsets), (0, 0))
    clists = jnp.pad(coarse_lists, extra, constant_values=groups * WIDE).reshape(steps, 1, WIDE)
    vmem = pl.BlockSpec(memory_space=pltpu.VMEM)
    return pl.pallas_call(
        far_kernel,
        out_shape=jax.ShapeDtypeStruct((coeffs, boxes), f32),
        in_specs=[vmem, vmem, pl.BlockSpec(memory_space=pl.ANY), vmem, vmem, vmem],
        out_specs=vmem,
        scratch_shapes=[
            pltpu.VMEM((coeffs, coeffs, offsets), bf16),
            pltpu.VMEM((offsets * ROWS, LANES), f32),
            pltpu.VMEM((STEP * LANES, 2 * WIDE), bf16),
            pltpu.VMEM((ROWS, 2 * WIDE), f32),
            pltpu.SemaphoreType.DMA((9 if coeffs % 9 == 0 else 1,)),
        ],
        compiler_params=pltpu.CompilerParams(vmem_limit_bytes=58 * 2**20),
        name="far",
    )(source, parents, translate.transpose(1, 2, 0), shift_down, leaf_lists, clists)


def exchange_kernel(
    leaf_ref, rows_ref, up_ref, atoms_ref, lists_ref, counts_ref,
    source_ref, parent_ref, near_ref,
    send_ref, land_ref, edge_ref, side_ref, entry_ref, send_sem, land_sem, edge_send_sem, edge_land_sem,
):
    coeffs, boxes = leaf_ref.shape
    slots = near_ref.shape[0]
    peers = send_ref.shape[0]
    tiles = boxes // LANES
    sizes = [lax.axis_size(axis) for axis in DEVICES]
    dom, slab, half = [lax.axis_index(axis) for axis in DEVICES]
    me = (dom * sizes[1] + slab) * sizes[2] + half

    def place(index):
        return {
            "dom": index // (sizes[1] * sizes[2]),
            "slab": (index // sizes[2]) % sizes[1],
            "half": index % sizes[2],
        }

    barrier = pltpu.get_barrier_semaphore()

    def greet(d, carry):
        pl.semaphore_signal(
            barrier, inc=1, device_id=place((me + d) % peers), device_id_type=pl.DeviceIdType.MESH
        )
        return carry

    lax.fori_loop(1, peers, greet, 0)

    own = jnp.concatenate([leaf_ref[...].astype(f32), jnp.zeros((LANES - coeffs, boxes), f32)], 0)
    packed = own.astype(bf16)
    up = up_ref[...]
    high = up.astype(bf16)
    low = (up - high.astype(f32)).astype(bf16)
    together = WIDE // CAP
    for j in range(peers // together):
        named = [rows_ref[p : p + 1, :] for p in range(j * together, (j + 1) * together)]
        hot = one_hot(jnp.concatenate(named, 1), boxes)
        part = jnp.transpose(jnp.dot(packed, hot, preferred_element_type=f32)).astype(bf16)
        for i in range(together):
            p = j * together + i
            send_ref[p, :CAP, :] = part[i * CAP : (i + 1) * CAP]
            send_ref[p, CAP : 2 * CAP, :] = high
            send_ref[p, 2 * CAP :, :] = low
    pl.semaphore_wait(barrier, peers - 1)

    def edge(side):
        lanes = pl.ds((1 - side) * (boxes - LANES), LANES)
        return pltpu.make_async_remote_copy(
            src_ref=atoms_ref.at[:, lanes], dst_ref=edge_ref.at[side],
            send_sem=edge_send_sem.at[side], recv_sem=edge_land_sem.at[side],
            device_id=place((me + 1 - 2 * side + peers) % peers),
            device_id_type=pl.DeviceIdType.MESH,
        )

    def sending(d):
        return pltpu.make_async_remote_copy(
            src_ref=send_ref.at[(me + d) % peers], dst_ref=land_ref.at[me],
            send_sem=send_sem.at[d], recv_sem=land_sem.at[d],
            device_id=place((me + d) % peers), device_id_type=pl.DeviceIdType.MESH,
        )

    def landing(d):
        sender = (me - d + peers) % peers
        return pltpu.make_async_remote_copy(
            src_ref=send_ref.at[sender], dst_ref=land_ref.at[sender],
            send_sem=send_sem.at[d], recv_sem=land_sem.at[d],
            device_id=place(sender), device_id_type=pl.DeviceIdType.MESH,
        )

    for side in range(2):
        edge(side).start()

    def start(d, carry):
        sending(d).start()
        return carry

    lax.fori_loop(1, peers, start, 0)
    land_ref[me] = send_ref[me]

    for side in range(2):
        edge(side).wait()
    below = jnp.where(me > 0, edge_ref[0], 0.0)
    above = jnp.where(me < peers - 1, edge_ref[1], 0.0)
    lower = lax.broadcasted_iota(jnp.int32, (1, LANES), 1) < LANES // 2
    for t in range(tiles):
        after = atoms_ref[:, (t + 1) * LANES : (t + 2) * LANES] if t + 1 < tiles else above
        before = atoms_ref[:, (t - 1) * LANES : t * LANES] if t else below
        side_ref[:, t * LANES : (t + 1) * LANES] = jnp.where(lower, after, before)

    for n in range(lists_ref.shape[0]):
        entry_ref[n] = lists_ref[n : n + 1, :]

    def step(n, totals):
        out = []
        for t in range(tiles):
            lanes = slice(t * LANES, (t + 1) * LANES)
            total = totals[t]
            entry = entry_ref[n, :, lanes]
            local = jnp.broadcast_to(entry - HALO, (8, LANES))
            inside = (local >= t * LANES) & (local < (t + 1) * LANES)
            lane = local & (LANES - 1)
            source = []
            for r in range(4 * slots // 8):
                rows = slice(8 * r, 8 * (r + 1))
                one = jnp.take_along_axis(atoms_ref[rows, lanes], lane, axis=1)
                two = jnp.take_along_axis(side_ref[rows, lanes], lane, axis=1)
                source.append(jnp.where(inside, one, two))
            source = jnp.concatenate(source, 0)
            charge = jnp.where(entry < boxes + 2 * HALO, source[3 * slots :], 0.0)
            target = [atoms_ref[k * slots : (k + 1) * slots, lanes] for k in range(3)]
            for b in range(slots):
                square = jnp.full((slots, LANES), softening, f32)
                for k in range(3):
                    diff = target[k] - source[k * slots + b : k * slots + b + 1]
                    square = square + diff * diff
                total = total + charge[b : b + 1] * lax.rsqrt(square)
            out.append(total)
        return tuple(out)

    zero = jnp.zeros((slots, LANES), f32)
    totals = lax.fori_loop(
        0, lists_ref.shape[0], step, (zero,) * tiles, unroll=unroll_of(lists_ref.shape[0])
    )
    slot = lax.broadcasted_iota(jnp.int32, (slots, LANES), 0)
    for t in range(tiles):
        lanes = slice(t * LANES, (t + 1) * LANES)
        near_ref[:, lanes] = jnp.where(slot < counts_ref[:, lanes], totals[t], 0.0)

    def finish(d, carry):
        sending(d).wait_send()
        landing(d).wait_recv()
        return carry

    lax.fori_loop(1, peers, finish, 0)

    def turned(j, kind):
        part = land_ref[j * together : (j + 1) * together, kind * CAP : (kind + 1) * CAP, :]
        return jnp.transpose(part.reshape(WIDE, LANES).astype(f32))[:ROWS]

    groups = peers // together
    source_ref[...] = jnp.concatenate(
        [own[:ROWS]] + [turned(j, 0) for j in range(groups)], 0
    ).astype(bf16)
    parent_ref[...] = jnp.concatenate(
        [turned(j, kind) for j in range(groups) for kind in (1, 2)], 0
    ).astype(bf16)


def exchange(leaf_multipoles, shift_up, export_rows, positions, charges, counts, near_lists):
    coeffs, boxes = leaf_multipoles.shape
    peers = export_rows.shape[1]
    slots = charges.shape[0] // boxes
    groups = peers * CAP // WIDE
    assert boxes // 8 == CAP
    children = leaf_multipoles.reshape(coeffs, boxes // 8, 8)
    parents = jnp.einsum("ckm,mpc->pk", shift_up, children, preferred_element_type=f32)
    parents = jnp.pad(parents, ((0, 0), (0, LANES - coeffs)))
    valid = jnp.arange(slots, dtype=jnp.int32)[:, None] < counts[None, :]
    charge = jnp.where(valid, charges.reshape(boxes, slots).T, 0.0)
    place = positions.reshape(3, boxes, slots).transpose(0, 2, 1).reshape(3 * slots, boxes)
    atoms = jnp.concatenate([place, charge], 0)
    vmem = pl.BlockSpec(memory_space=pltpu.VMEM)
    source, parent, potential = pl.pallas_call(
        exchange_kernel,
        out_shape=(
            jax.ShapeDtypeStruct(((groups + 1) * ROWS, WIDE), bf16),
            jax.ShapeDtypeStruct((groups * 2 * ROWS, WIDE), bf16),
            jax.ShapeDtypeStruct((slots, boxes), f32),
        ),
        in_specs=[vmem] * 6,
        out_specs=(vmem,) * 3,
        scratch_shapes=[
            pltpu.VMEM((peers, 3 * CAP, LANES), bf16),
            pltpu.VMEM((peers, 3 * CAP, LANES), bf16),
            pltpu.VMEM((2, 4 * slots, LANES), f32),
            pltpu.VMEM((4 * slots, boxes), f32),
            pltpu.VMEM((near_lists.shape[0], 1, boxes), jnp.int32),
            pltpu.SemaphoreType.DMA((peers,)),
            pltpu.SemaphoreType.DMA((peers,)),
            pltpu.SemaphoreType.DMA((2,)),
            pltpu.SemaphoreType.DMA((2,)),
        ],
        compiler_params=pltpu.CompilerParams(
            collective_id=0, has_side_effects=True, vmem_limit_bytes=58 * 2**20
        ),
        name="exchange",
    )(
        leaf_multipoles, export_rows[0], parents, atoms,
        near_lists, counts[None, :],
    )
    return source, parent, potential.T.reshape(boxes * slots)


def body(
    leaf_multipoles, translate, shift_up, shift_down, export_rows, leaf_lists, coarse_lists,
    positions, charges, counts, near_lists,
):
    source, parents, near_potential = exchange(
        leaf_multipoles, shift_up, export_rows, positions, charges, counts, near_lists
    )
    local_field = far_sum(source, parents, translate, shift_down, leaf_lists, coarse_lists)
    return (local_field, near_potential)


def solution(mesh):
    every = ("rep",) + DEVICES
    in_specs = (
        P(None, every), P(), P(), P(), P(every, None, None), P(None, every), P(None, every),
        P(None, every), P(every), P(every), P(None, every),
    )
    out_specs = (P(None, every), P(every))
    return jax.shard_map(body, mesh=mesh, in_specs=in_specs, out_specs=out_specs, check_vma=False)
```
